32 devices in a mesh: rep: 4 (over z), fsdp: 8 (over y, x, core).
Axes of the slice: x: 2, y: 2, z: 4, core: 2. Of those that a mesh axis runs over, the one named last changes fastest.
Arguments:
- acts: bfloat16 [4, 4096, 3072], P('rep', 'fsdp'), may hold values from -6 to 6
- cotangent: bfloat16 [4, 4096, 512], P('rep', 'fsdp'), may hold values from -0.09375 to 0.09375
- nonfinite_row_mask: int32 [4, 3072], P('rep', 'fsdp'), may hold values from 0 to 1, as said below
- params: float32 [4, 3072, 512], P('rep', 'fsdp'), may hold values from -6 to 6
- adam_first_state: float32 [4, 3072, 512], P('rep', 'fsdp'), may hold values from -6 to 6
- adam_second_state: float32 [4, 3072, 512], P('rep', 'fsdp'), may hold values from 0.2 to 4
- anchor: float32 [3072, 512], P('fsdp'), may hold values from -6 to 6
- momentum: float32 [3072, 512], P('fsdp'), may hold values from -3 to 3
Outputs:
- anchor_next: float32 [3072, 512], P('fsdp')
- momentum_next: float32 [3072, 512], P('fsdp')
- first_next: float32 [4, 3072, 512], P('rep', 'fsdp')
- second_next: float32 [4, 3072, 512], P('rep', 'fsdp')
The draws below stay inside these ranges and needn't reach their ends.
Inputs may be any that keep to these rules, and one draw needn't show every extreme that they name: `nonfinite_row_mask`: exactly one replica has a marked row, and it has exactly one; all other replicas have none.
All inputs are finite; a program needn't handle non-finite values.
Results may differ from the reference program's by a relative error of at most 0.0003.
Values may be sent and summed in bfloat16 or wider, within the bound.
A program may use at most 128 MiB of HBM per device.

```python
import math
import jax
import jax.numpy as jnp
from jax import lax

D = 3072
KV = 512
TOKENS = 4096
REPS = 4


def draw_nonfinite_row_mask(key, part):
    keys = jax.random.split(jax.random.fold_in(key, 17), 2)
    position = jax.random.randint(keys[0], (), 0, D)
    chosen = jax.random.randint(keys[1], (), 0, REPS)
    replicas = jnp.arange(REPS)
    marks = (replicas[:, None] == chosen) & (jnp.arange(D)[None, :] == position)
    return marks.astype(jnp.int32)


def spiked(drawn, own_key, source, target, parts, factor):
    owner, partner = [(jnp.arange(drawn.shape[dim]) // (drawn.shape[dim] // parts)).reshape([-1 if axis == dim else 1 for axis in range(drawn.ndim)]) for dim in (source, target)]
    chosen = jax.random.permutation(own_key, parts)[partner]
    strong = (owner == chosen) | (owner == (partner + parts // 2) % parts)
    return jnp.where(strong, factor * drawn, drawn)


def shard_levels(own_key, shape, cuts, low, top_value):
    def one(dim, parts):
        steps = jax.random.uniform(jax.random.fold_in(jax.random.fold_in(own_key, 6), dim), (parts,), jnp.float32, low / len(cuts), top_value / len(cuts))
        return jnp.repeat(jnp.exp(steps), shape[dim] // parts).reshape((-1,) + (1,) * (len(shape) - dim - 1))

    loudness = one(*cuts[0])
    for cut in cuts[1:]:
        loudness = loudness * one(*cut)
    return loudness


def bell_draw(own_key, extent, scale, limit, cuts=(), dtype=jnp.bfloat16):
    values = scale * jax.random.normal(own_key, extent, jnp.float32)
    if cuts:
        values = values * shard_levels(own_key, extent, cuts, -0.22, 0.18)
    return jnp.clip(values, -limit, limit).astype(dtype)


def gaussian_with(stream_key, shape, spread, limit, pieces, heavy, kind=jnp.bfloat16):
    entries = spread * jax.random.normal(stream_key, shape, jnp.float32)
    if pieces:
        entries = entries * shard_levels(stream_key, shape, pieces, -0.22, 0.18)
    return jnp.clip(spiked(entries, jax.random.fold_in(stream_key, 3), *heavy), -limit, limit).astype(kind)


def setup_inputs(seed: int = 0) -> dict:
    seeds = jax.random.split(jax.random.key(seed), 9)
    acts = gaussian_with(seeds[0], (REPS, TOKENS, D), 1.0, 6.0, ((0, 4), (1, 8)), (1, 2, 8, 2.0))
    cotangent = bell_draw(seeds[1], (REPS, TOKENS, KV), TOKENS ** -0.5, 0.09375, ((0, 4), (1, 8)))
    nonfinite_row_mask = draw_nonfinite_row_mask(jax.random.fold_in(seeds[8], 71), 0)
    params = bell_draw(seeds[3], (REPS, D, KV), 1.0, 6.0, ((0, 4), (1, 8)), jnp.float32)
    adam_first_state = bell_draw(seeds[4], (REPS, D, KV), 1.0, 6.0, ((0, 4), (1, 8)), jnp.float32)
    adam_second_state = jnp.clip(jnp.exp(math.log(4.0) - 2.9957323 * jax.random.uniform(seeds[5], (REPS, D, KV), jnp.float32) ** shard_levels(seeds[5], (REPS, D, KV), ((0, 4), (1, 8)), -0.2, 0.2)), 0.2, 4.0)
    anchor = bell_draw(seeds[6], (D, KV), 1.0, 6.0, ((0, 8),), jnp.float32)
    momentum = bell_draw(seeds[7], (D, KV), 0.5, 3.0, ((0, 8),), jnp.float32)
    return dict(acts=acts, cotangent=cotangent, nonfinite_row_mask=nonfinite_row_mask, params=params, adam_first_state=adam_first_state, adam_second_state=adam_second_state, anchor=anchor, momentum=momentum)


corr_first = 1.0 - 0.9 ** 10
corr_second = 1.0 - 0.95 ** 10

def replica_grad(pair):
    inputs, upstream = pair
    return lax.dot_general(inputs, upstream, (((0,), (0,)), ((), ())), preferred_element_type=jnp.float32)

def reference(acts, cotangent, nonfinite_row_mask, params, adam_first_state, adam_second_state, anchor, momentum):
    gradient_value = lax.map(replica_grad, (acts, cotangent))
    corrupted_gradient = jnp.where((nonfinite_row_mask == 1)[:, :, None], jnp.float32(jnp.nan), gradient_value)
    nonfinite_flag = jnp.any(jnp.isnan(corrupted_gradient), axis=(1, 2))
    keep = jnp.logical_not(nonfinite_flag)
    first_state_value = 0.9 * adam_first_state + 0.1 * corrupted_gradient
    second_state_value = 0.95 * adam_second_state + 0.05 * corrupted_gradient * corrupted_gradient
    update = first_state_value / corr_first / (jnp.sqrt(second_state_value / corr_second) + 1e-08)
    inner = params - 0.1 * (update + 0.1 * params)
    pseudo = anchor[None] - inner
    first_next = jnp.where(keep[:, None, None], first_state_value, adam_first_state)
    second_next = jnp.where(keep[:, None, None], second_state_value, adam_second_state)
    total = lax.optimization_barrier(jnp.sum(jnp.where(keep[:, None, None], pseudo, jnp.float32(0.0)), axis=0))
    count = jnp.sum(keep.astype(jnp.float32))
    average = total / count
    momentum_next = 0.9 * momentum + average
    anchor_next = anchor - 0.7 * (average + 0.9 * momentum_next)
    return (anchor_next, momentum_next, first_next, second_next)
```

```python
import jax
import jax.numpy as jnp
from jax import lax
from jax.experimental import pallas as pl
from jax.experimental.pallas import tpu as pltpu
from jax.sharding import PartitionSpec as P

corr_first = 1.0 - 0.9**10
corr_second = 1.0 - 0.95**10


def body(
    acts,
    cotangent,
    nonfinite_row_mask,
    params,
    adam_first_state,
    adam_second_state,
    anchor,
    momentum,
):
    inputs = acts[0]
    upstream = cotangent[0]
    contract = (((0,), (0,)), ((), ()))
    gradient_value = lax.psum_scatter(
        lax.dot_general(inputs, upstream, contract, preferred_element_type=jnp.float32),
        "fsdp",
        scatter_dimension=0,
        tiled=True,
    )
    corrupted_gradient = jnp.where(
        (nonfinite_row_mask[0] == 1)[:, None], jnp.float32(jnp.nan), gradient_value
    )
    replica_nonfinite = jnp.any(jnp.isnan(corrupted_gradient)).astype(jnp.int32)
    first_state_value = 0.9 * adam_first_state[0] + 0.1 * corrupted_gradient
    second_state_value = (
        0.95 * adam_second_state[0] + 0.05 * corrupted_gradient * corrupted_gradient
    )
    update = first_state_value / corr_first / (jnp.sqrt(second_state_value / corr_second) + 1e-08)
    inner = params[0] - 0.1 * (update + 0.1 * params[0])
    pseudo = anchor - inner
    replica_bad = lax.pmax(replica_nonfinite, "fsdp")
    keep = replica_bad == 0
    share = jnp.where(keep, pseudo, jnp.float32(0.0))
    total, count = lax.psum((share, keep.astype(jnp.float32)), "rep")
    average = total / count
    momentum_next = 0.9 * momentum + average
    anchor_next = anchor - 0.7 * (average + 0.9 * momentum_next)
    first_next = jnp.where(keep, first_state_value, adam_first_state[0])[None]
    second_next = jnp.where(keep, second_state_value, adam_second_state[0])[None]
    return (anchor_next, momentum_next, first_next, second_next)


NC = 4
MESH = pl.DeviceIdType.MESH
LIMIT = 7.5
UNIT = 32767.0 / LIMIT


def kernel(
    acts, cot, mask, params, first, second, anchor, momentum,
    o_anchor, o_mom, o_first, o_second,
    a_buf, c_buf, p_buf, m_buf, v_buf, an_buf, mo_buf,
    send_g, own_g, recv_d, recv_raw, recv_sum, sc_out, sc_sum, sc_in, flag_out, flag_in,
    z_own, z_mid, z_fin, r_edge, r_mid, r_fin,
    load_sem, core_s, core_r, flag_s, flag_r,
    d_s, d_r, raw_s, raw_r, sum_s, sum_r, sc_s, sc_r, zs, zr, out_sem,
):
    rows = p_buf.shape[0]
    tok = acts.shape[0]
    ch = rows // NC
    h = ch // 2
    kv = p_buf.shape[1]
    rep = lax.axis_index("rep")
    f = lax.axis_index("fsdp")
    c = lax.rem(f, 2)
    x = lax.rem(lax.div(f, 2), 2)
    y = lax.div(f, 4)

    def at(j):
        yy = 1 - y if j & 4 else y
        xx = 1 - x if j & 2 else x
        cc = 1 - c if j & 1 else c
        return yy * 4 + xx * 2 + cc

    loads = []

    def load(src, dst, i):
        cp = pltpu.make_async_copy(src, dst, load_sem.at[i])
        cp.start()
        loads.append(cp)

    order = (6, 2, 4, 0)
    load(cot, c_buf.at[pl.ds(0, tok)], 0)
    for i, j in enumerate(order):
        load(acts.at[:, pl.ds(pl.multiple_of(at(j) * rows, 128), rows)], a_buf.at[i, pl.ds(0, tok)], 1 + i)
    for i, (s, d) in enumerate(((params, p_buf), (first, m_buf), (second, v_buf), (anchor, an_buf), (momentum, mo_buf))):
        load(s, d, 5 + i)

    zmate = lax.div(rep, 2) * 2 + (1 - lax.rem(rep, 2))
    zmid = 3 - rep
    edge = (rep == 0) | (rep == 3)
    inner = jnp.logical_not(edge)

    barrier = pltpu.get_barrier_semaphore()
    for j in range(1, 8):
        pl.semaphore_signal(barrier, inc=1, device_id=(rep, at(j)), device_id_type=MESH)
    pl.semaphore_signal(barrier, inc=1, device_id=(zmate, f), device_id_type=MESH)
    pl.semaphore_signal(barrier, inc=1, device_id=(zmid, f), device_id_type=MESH)
    pl.semaphore_wait(barrier, 9)

    sends = []

    def remote(src, dst, s, r, dev):
        return pltpu.make_async_remote_copy(
            src_ref=src, dst_ref=dst, send_sem=s, recv_sem=r, device_id=dev, device_id_type=MESH
        )

    core = [remote(cot, c_buf.at[pl.ds(tok, tok)], core_s.at[0], core_r.at[0], (rep, at(1)))]
    for i, j in enumerate(order):
        core.append(
            remote(
                acts.at[:, pl.ds(pl.multiple_of(at(j ^ 1) * rows, 128), rows)],
                a_buf.at[i, pl.ds(tok, tok)],
                core_s.at[1 + i], core_r.at[1 + i], (rep, at(1)),
            )
        )
    for cp in core:
        cp.start()

    flag_out[...] = jnp.broadcast_to(jnp.max(mask[...], axis=1, keepdims=True), flag_out.shape)
    flags = [
        remote(flag_out, flag_in.at[j], flag_s.at[j], flag_r.at[j], (rep, at(j))) for j in range(1, 8)
    ]
    for cp in flags:
        cp.start()

    def product(i):
        loads[1 + i].wait()
        core[1 + i].wait_recv()
        return lax.dot_general(
            a_buf[i], c_buf[...], (((0,), (0,)), ((), ())), preferred_element_type=jnp.float32
        )

    def half(k, b):
        return pl.ds(k * ch + b * h, h)

    peers = ((rep, at(2)), (rep, at(4)))
    diag, raw, summed = {}, {}, {}
    for k in range(NC):
        for b in range(2):
            diag[k, b] = remote(
                send_g.at[0, half(k, b)], recv_d.at[b, k], d_s.at[b, k], d_r.at[b, k], peers[b]
            )
            raw[k, b] = remote(
                send_g.at[1 + b, half(k, b)], recv_raw.at[b, k], raw_s.at[b, k], raw_r.at[b, k], peers[b]
            )
            summed[k, b] = remote(
                send_g.at[1 + b, half(k, 1 - b)], recv_sum.at[b, k], sum_s.at[b, k], sum_r.at[b, k], peers[b]
            )

    scale = {}
    for b in range(2):
        for n, src in enumerate((sc_out.at[0], sc_out.at[1 + b], sc_sum.at[b])):
            scale[n, b] = remote(src, sc_in.at[n, b], sc_s.at[n, b], sc_r.at[n, b], peers[b])

    def wide(top):
        return jnp.broadcast_to(top, (1, kv))

    def code(values, top):
        return jnp.round(values * (32767.0 / wide(top))).astype(jnp.int32).astype(jnp.int16)

    def decode(codes, top):
        return codes.astype(jnp.int32).astype(jnp.float32) * (wide(top) * (1.0 / 32767.0))

    def pack(i):
        g = product(i)
        top = jnp.max(jnp.max(jnp.abs(g), axis=0, keepdims=True), axis=1, keepdims=True)
        top = jnp.maximum(top, 1e-30)
        sc_out[i] = jnp.broadcast_to(top, (8, 128))
        send_g[i] = code(g, top)

    def start(group, k):
        if k < NC:
            group[k, 0].start()
            group[k, 1].start()

    loads[0].wait()
    core[0].wait_recv()
    pack(0)
    scale[0, 0].start()
    scale[0, 1].start()
    start(diag, 0)
    start(diag, 1)
    pack(1)
    scale[1, 0].start()
    raw[0, 0].start()
    pack(2)
    scale[1, 1].start()
    raw[0, 1].start()
    mine, came, both = [], [], []
    for b in range(2):
        scale[0, 1 - b].wait_recv()
        mine.append(sc_out[1 + b][0:1, 0:1])
        came.append(sc_in[0, 1 - b][0:1, 0:1])
        both.append(mine[b] + came[b])
        sc_sum[b] = jnp.broadcast_to(both[b], (8, 128))
        scale[2, b].start()

    def forward(k):
        for b in range(2):
            diag[k, 1 - b].wait_recv()
            r = half(k, 1 - b)
            send_g[1 + b, r] = code(
                decode(send_g[1 + b, r], mine[b]) + decode(recv_d[1 - b, k], came[b]), both[b]
            )
            summed[k, b].start()

    forward(0)
    start(raw, 1)
    start(diag, 2)
    own_g[...] = product(3)
    for i in range(5):
        loads[5 + i].wait()

    for b in range(2):
        scale[1, b].wait_recv()
        scale[2, b].wait_recv()
    raw_top = [sc_in[1, b][0:1, 0:1] for b in range(2)]
    sum_top = [sc_in[2, b][0:1, 0:1] for b in range(2)]
    bad = jnp.max(flag_out[...])
    for j in range(1, 8):
        flags[j - 1].wait_recv()
        bad = jnp.maximum(bad, jnp.max(flag_in[j]))
    keep = bad == 0
    count = 3.0

    def zcopy(n, src, dst, k, dev):
        return remote(src.at[k], dst.at[k], zs.at[n, k], zr.at[n, k], dev)

    to_inner = [zcopy(0, z_own, r_edge, k, (zmate, f)) for k in range(NC)]
    across = [zcopy(1, z_mid, r_mid, k, (zmid, f)) for k in range(NC)]
    to_edge = [zcopy(2, z_fin, r_fin, k, (zmate, f)) for k in range(NC)]
    outs = []

    def put(src, dst, k, n):
        r = pl.ds(k * ch, ch)
        cp = pltpu.make_async_copy(src.at[r], dst.at[r], out_sem.at[n, k])
        cp.start()
        outs.append(cp)

    def adam(k):
        for b in range(2):
            raw[k, b].wait_recv()
            summed[k, 1 - b].wait_recv()
            r = half(k, b)
            g = own_g[r] + decode(recv_raw[b, k], raw_top[b]) + decode(recv_sum[1 - b, k], sum_top[1 - b])
            m0, v0, p = m_buf[r], v_buf[r], p_buf[r]
            m = 0.9 * m0 + 0.1 * g
            v = 0.95 * v0 + 0.05 * g * g
            update = m / corr_first / (jnp.sqrt(v / corr_second) + 1e-08)
            new = jnp.where(keep, p - 0.1 * (update + 0.1 * p), 0.0) * UNIT
            p_buf[r] = new
            z_own[k, pl.ds(b * h, h)] = jnp.round(new).astype(jnp.int32).astype(jnp.int16)
            m_buf[r] = jnp.where(keep, m, m0)
            v_buf[r] = jnp.where(keep, v, v0)

        @pl.when(edge)
        def _():
            to_inner[k].start()

        put(m_buf, o_first, k, 0)
        put(v_buf, o_second, k, 1)

    def pair(k):
        @pl.when(inner)
        def _():
            to_inner[k].wait_recv()
            s = p_buf[pl.ds(k * ch, ch)] + r_edge[k].astype(jnp.int32).astype(jnp.float32)
            z_mid[k] = jnp.round(s * 0.5).astype(jnp.int32).astype(jnp.int16)
            across[k].start()

    def finish(k):
        @pl.when(inner)
        def _():
            across[k].wait_recv()
            s = (z_mid[k].astype(jnp.int32) + r_mid[k].astype(jnp.int32)).astype(jnp.float32)
            z_fin[k] = jnp.round(s * (2.0 / 3.0)).astype(jnp.int32).astype(jnp.int16)
            to_edge[k].start()
            r_fin[k] = z_fin[k]

        @pl.when(edge)
        def _():
            to_edge[k].wait_recv()

        r = pl.ds(k * ch, ch)
        total = r_fin[k].astype(jnp.int32).astype(jnp.float32) * (3.0 / UNIT)
        a = an_buf[r]
        average = a - total / count
        mo = 0.9 * mo_buf[r] + average
        an_buf[r] = a - 0.7 * (average + 0.9 * mo)
        mo_buf[r] = mo
        put(an_buf, o_anchor, k, 2)
        put(mo_buf, o_mom, k, 3)

    for k in range(NC + 2):
        if k + 1 < NC:
            forward(k + 1)
            if k + 2 < NC:
                start(raw, k + 2)
            start(diag, k + 3)
        if k < NC:
            adam(k)
        if 0 <= k - 1 < NC:
            pair(k - 1)
        if 0 <= k - 2 < NC:
            finish(k - 2)

    for cp in core + flags:
        cp.wait_send()
    for group in (diag, raw, summed, scale):
        for cp in group.values():
            cp.wait_send()
    for k in range(NC):

        @pl.when(edge)
        def _():
            to_inner[k].wait_send()

        @pl.when(inner)
        def _():
            across[k].wait_send()
            to_edge[k].wait_send()

    for cp in outs:
        cp.wait()


def fused(acts, cotangent, nonfinite_row_mask, params, first, second, anchor, momentum):
    rows, kv = anchor.shape
    tok = acts.shape[1]
    ch = rows // NC
    h = ch // 2
    bf, f32, dma = jnp.bfloat16, jnp.float32, pltpu.SemaphoreType.DMA
    block = jax.ShapeDtypeStruct((rows, kv), f32)
    hbm = pl.BlockSpec(memory_space=pl.ANY)
    out = pl.pallas_call(
        kernel,
        out_shape=[block] * 4,
        in_specs=[hbm, hbm, pl.BlockSpec(memory_space=pltpu.VMEM)] + [hbm] * 5,
        out_specs=[hbm] * 4,
        scratch_shapes=[
            pltpu.VMEM((4, 2 * tok, rows), bf),
            pltpu.VMEM((2 * tok, kv), bf),
        ]
        + [pltpu.VMEM((rows, kv), f32)] * 5
        + [
            pltpu.VMEM((3, rows, kv), jnp.int16),
            pltpu.VMEM((rows, kv), f32),
            pltpu.VMEM((2, NC, h, kv), jnp.int16),
            pltpu.VMEM((2, NC, h, kv), jnp.int16),
            pltpu.VMEM((2, NC, h, kv), jnp.int16),
            pltpu.VMEM((3, 8, 128), f32),
            pltpu.VMEM((2, 8, 128), f32),
            pltpu.VMEM((3, 2, 8, 128), f32),
            pltpu.VMEM((8, 128), jnp.int32),
            pltpu.VMEM((8, 8, 128), jnp.int32),
        ]
        + [pltpu.VMEM((NC, ch, kv), jnp.int16)] * 6
        + [dma((10,)), dma((5,)), dma((5,)), dma((8,)), dma((8,))]
        + [dma((2, NC))] * 6
        + [dma((3, 2)), dma((3, 2)), dma((3, NC)), dma((3, NC)), dma((4, NC))],
        compiler_params=pltpu.CompilerParams(
            collective_id=0, has_side_effects=True, vmem_limit_bytes=40 * 2**20
        ),
        cost_estimate=pl.CostEstimate(
            flops=2 * 8 * rows * tok * kv, bytes_accessed=12 * 2**20, transcendentals=rows * kv
        ),
    )(acts[0], cotangent[0], nonfinite_row_mask, params[0], first[0], second[0], anchor, momentum)
    return out[0], out[1], out[2][None], out[3][None]


def solution(mesh):
    in_specs = (
        P("rep", "fsdp", None),
        P("rep", "fsdp", None),
        P("rep", "fsdp"),
        P("rep", "fsdp", None),
        P("rep", "fsdp", None),
        P("rep", "fsdp", None),
        P("fsdp", None),
        P("fsdp", None),
    )
    out_specs = (P("fsdp", None), P("fsdp", None), P("rep", "fsdp", None), P("rep", "fsdp", None))
    block = mesh.shape["rep"] == 4 and mesh.shape["fsdp"] == 8
    return jax.shard_map(
        fused if block else body, mesh=mesh, in_specs=in_specs, out_specs=out_specs, check_vma=False
    )
```
